32 devices in a mesh: groups: 2 (over y), node: 4 (over z), local: 2 (over x), sub: 2 (over core).
Axes of the slice: x: 2, y: 2, z: 4, core: 2. Of those that a mesh axis runs over, the one named last changes fastest.
Arguments:
- tokens: bfloat16 [256, 3584], P(('groups', 'node', 'local', 'sub')), parts along dimension 0, may hold values from -6 to 6
- ids: int32 [256, 8], P(('groups', 'node', 'local', 'sub')), parts along dimension 0, may hold values from 0 to 7, as said below
- scores: float32 [256, 8], P(('groups', 'node', 'local', 'sub')), parts along dimension 0, may hold values from -6 to 6
- gate_w: bfloat16 [8, 3584, 2048], P('node', None, ('local', 'sub')), may hold values from -0.09375 to 0.09375
- up_w: bfloat16 [8, 3584, 2048], P('node', None, ('local', 'sub')), may hold values from -0.09375 to 0.09375
- down_w: bfloat16 [8, 2048, 3584], P('node', None, ('local', 'sub')), may hold values from -0.125 to 0.125
Outputs:
- combined: bfloat16 [256, 3584], P(('groups', 'node', 'local', 'sub')), parts along dimension 0
The draws below stay inside these ranges and needn't reach their ends.
There are 2 independent parts, one for each index of `groups`. The reference program is written for one: setup_inputs(seed, part) draws one part's arguments, and reference() takes and returns one part's arrays. A program takes and returns all parts, laid end to end along the dimension named above; an argument that names none is the same for every part. Nothing has to cross between parts.
Inputs may be any that keep to these rules, and one draw needn't show every extreme that they name: `ids`: each token names 8 different experts. Of the 8 tokens of one device (an aligned block of rows), at most 8 name any one expert, and in every draw one expert is named by exactly 8 tokens of every device.
All inputs are finite; a program needn't handle non-finite values.
Results may differ from the reference program's by a relative error of at most 0.0058.
Values may be sent and summed in bfloat16 or wider, within the bound.
No kernel may reach another device: no remote copies, remote signals or barrier semaphores. Data moves between devices by JAX's collectives and lax.ppermute only.
A program may use at most 192 MiB of HBM per device.

```python
import jax
import jax.numpy as jnp
from jax import lax

D = 3584
FF = 2048
K = 8
TOK_DEV = 8
EXPERTS = 8
CAP = 8
TOKENS = 128


def draw_ids(key, part):
    key = jax.random.fold_in(key, 11)
    blocks = TOKENS // TOK_DEV
    stride = (K + CAP - 1) // CAP
    hot_expert = jax.random.randint(jax.random.fold_in(key, 1), (), 0, EXPERTS)
    order_keys = jax.random.split(jax.random.fold_in(key, 2), blocks)
    orders = jax.vmap(lambda block_key: jax.random.permutation(block_key, EXPERTS))(order_keys)
    anchor = stride * (CAP - 1) % EXPERTS
    columns = jnp.arange(EXPERTS)[None, :]
    hot_place = jnp.argmax(orders == hot_expert, axis=1)
    anchor_value = orders[:, anchor]
    orders = jnp.where(columns == anchor, hot_expert, jnp.where(columns == hot_place[:, None], anchor_value[:, None], orders))
    row_index = jnp.arange(TOK_DEV)[:, None]
    pick_index = jnp.arange(K)[None, :]
    positions = (stride * row_index + pick_index) % EXPERTS
    chosen = orders[:, positions]
    row_keys = jax.random.split(jax.random.fold_in(key, 3), blocks)
    shuffles = jax.vmap(lambda block_key: jax.random.permutation(block_key, TOK_DEV))(row_keys)
    chosen = jnp.take_along_axis(chosen, shuffles[:, :, None], axis=1)
    return chosen.reshape(TOKENS, K).astype(jnp.int32)


def levels(key, shape, pieces, low, top_value):
    def one(axis_at, parts):
        heights = jax.random.uniform(jax.random.fold_in(jax.random.fold_in(key, 6), axis_at), (parts,), jnp.float32, low / len(pieces), top_value / len(pieces))
        return jnp.repeat(jnp.exp(heights), shape[axis_at] // parts).reshape((-1,) + (1,) * (len(shape) - axis_at - 1))

    gain = one(*pieces[0])
    for cut in pieces[1:]:
        gain = gain * one(*cut)
    return gain


def scatter_about(rng, shape, spread, bound, shards=(), kind=jnp.bfloat16):
    gain = levels(rng, shape, shards, -0.22, 0.18) if shards else 1.0
    result = jax.random.normal(rng, shape, jnp.float32) * spread * gain
    return jnp.minimum(jnp.maximum(result, -bound), bound).astype(kind)


def setup_inputs(seed: int = 0, part: int = 0) -> dict:
    splits = jax.random.split(jax.random.key(seed), 7)
    own_keys = jax.random.split(jax.random.fold_in(splits[6], part), 7)
    return {
        "tokens": scatter_about(own_keys[0], (TOKENS, D), 1.0, 6.0, ((0, 16),)),
        "ids": draw_ids(jax.random.fold_in(jax.random.fold_in(splits[6], part), 71), part),
        "scores": scatter_about(own_keys[2], (TOKENS, K), 1.5, 6.0, ((0, 16),), jnp.float32),
        "gate_w": scatter_about(splits[3], (EXPERTS, D, FF), D ** -0.5, 0.09375, ((0, 4), (2, 4))),
        "up_w": scatter_about(splits[4], (EXPERTS, D, FF), D ** -0.5, 0.09375, ((0, 4), (2, 4))),
        "down_w": scatter_about(splits[5], (EXPERTS, FF, D), FF ** -0.5, 0.125, ((0, 4), (2, 4))),
    }


route_scale = 2.827


def reference(tokens, ids, scores, gate_w, up_w, down_w):
    blocks = TOKENS // TOK_DEV
    total_rows = TOKENS * K
    flat_experts = ids.reshape(-1)
    one_hot = (flat_experts[:, None] == jnp.arange(EXPERTS, dtype=jnp.int32)[None, :]).astype(jnp.int32)
    per_block = one_hot.reshape(blocks, TOK_DEV * K, EXPERTS)
    before = (jnp.cumsum(per_block, axis=1) - per_block).reshape(total_rows, EXPERTS)
    slot_rank = jnp.sum(before * one_hot, axis=1).astype(jnp.int32)
    block_of = jnp.arange(total_rows, dtype=jnp.int32) // (TOK_DEV * K)
    place = ((flat_experts * blocks + block_of) * CAP + slot_rank).astype(jnp.int32)
    table = jnp.full((EXPERTS * blocks * CAP,), total_rows, jnp.int32)
    table = table.at[place].set(jnp.arange(total_rows, dtype=jnp.int32))
    padded_tokens = jnp.concatenate([tokens, jnp.zeros((1, D), jnp.bfloat16)], axis=0)
    token_of = (table // K).astype(jnp.int32)

    def one_expert(operands):
        gate_m, up_m, down_m, rows_index = operands
        inputs = padded_tokens[rows_index]
        gate_part = jnp.dot(inputs, gate_m, preferred_element_type=jnp.float32)
        up_part = jnp.dot(inputs, up_m, preferred_element_type=jnp.float32)
        hidden = (jax.nn.silu(gate_part) * up_part).astype(jnp.bfloat16)
        return jnp.dot(hidden, down_m, preferred_element_type=jnp.float32).astype(jnp.bfloat16)

    outputs = lax.map(one_expert, (gate_w, up_w, down_w, token_of.reshape(EXPERTS, blocks * CAP)))
    scattered = jnp.zeros((total_rows + 1, D), jnp.bfloat16).at[table].set(outputs.reshape(-1, D))
    picked = scattered[:total_rows].astype(jnp.float32).reshape(TOKENS, K, D)
    sigmoid_vals = jax.nn.sigmoid(scores)
    share = route_scale * sigmoid_vals / jnp.sum(sigmoid_vals, axis=1, keepdims=True)
    return jnp.sum(share[:, :, None] * picked, axis=1).astype(jnp.bfloat16)
```

```python
import functools

import jax
import jax.numpy as jnp
from jax import lax
from jax.experimental import pallas as pl
from jax.experimental.pallas import tpu as pltpu
from jax.sharding import PartitionSpec as P

route_scale = 2.827
LANES = 128
f32, bf16 = jnp.float32, jnp.bfloat16
VMEM = pl.BlockSpec(memory_space=pltpu.VMEM)


def swap(x, axis, k):
    return lax.ppermute(x, axis, [(i, i ^ k) for i in range(lax.axis_size(axis))])


def call(kernel, out_shape, n_in, flops=0, size=0, vmem=16):
    return pl.pallas_call(
        kernel,
        out_shape=out_shape,
        in_specs=[VMEM] * n_in,
        out_specs=jax.tree.map(lambda _: VMEM, out_shape),
        compiler_params=pltpu.CompilerParams(vmem_limit_bytes=vmem << 20),
        cost_estimate=pl.CostEstimate(flops=flops, bytes_accessed=size, transcendentals=0),
    )


def pack_kernel(experts, tok_ref, ids_ref, scores_ref, out_ref):
    rows, features = tok_ref.shape
    extra = out_ref.shape[1] - features
    out_ref[:, :features] = tok_ref[...]
    gate = 1.0 / (1.0 + jnp.exp(-scores_ref[...]))
    share = route_scale * gate / jnp.sum(gate, axis=1, keepdims=True)
    column = lax.broadcasted_iota(jnp.int32, (rows, extra), 1)
    expert, term = column % experts, column // experts
    weight = jnp.zeros((rows, extra), f32)
    for k in range(ids_ref.shape[1]):
        weight += jnp.where(ids_ref[:, k : k + 1] == expert, share[:, k : k + 1], 0.0)
    first = weight.astype(bf16).astype(f32)
    second = (weight - first).astype(bf16).astype(f32)
    third = weight - first - second
    terms = jnp.where(term == 0, first, jnp.where(term == 1, second, jnp.where(term == 2, third, 0.0)))
    out_ref[:, features:] = terms.astype(bf16)


def hidden_kernel(e, experts, features, *refs):
    *blocks, gate_ref, up_ref, out_ref = refs
    local_experts = gate_ref.shape[0]
    x = jnp.concatenate([b[:, :features] for b in blocks], axis=0)
    tail = jnp.concatenate([b[:, features:] for b in blocks], axis=0).astype(f32)
    column = lax.broadcasted_iota(jnp.int32, tail.shape, 1)
    mine = lax.axis_index("node") * local_experts + e
    keep = (column % experts == mine) & (column < 3 * experts)
    weight = jnp.sum(jnp.where(keep, tail, 0.0), axis=1, keepdims=True)
    gate = jnp.dot(x, gate_ref[e], preferred_element_type=f32)
    up = jnp.dot(x, up_ref[e], preferred_element_type=f32)
    out_ref[...] = (gate / (1.0 + jnp.exp(-gate)) * up * weight).astype(bf16)


def down_kernel(local, sub, nodes, local_experts, *refs):
    n_slices = local * sub
    hidden, (down_ref, *outs) = refs[: local_experts * n_slices], refs[local_experts * n_slices :]
    tokens, depth = hidden[0].shape
    block = tokens // n_slices
    me = lax.axis_index("local") * sub + lax.axis_index("sub")
    total = jnp.zeros((tokens, down_ref.shape[2]), f32)
    for r in range(n_slices):
        s, x = divmod(r, local)
        rows = pl.ds(pl.multiple_of((me ^ (x * sub + s)) * depth, depth), depth)
        for e in range(local_experts):
            ref = hidden[e * n_slices + r]
            h = jnp.concatenate(
                [ref[pl.ds((b ^ r) * block, block), :] for b in range(n_slices)], axis=0
            )
            total += jnp.dot(h, down_ref[e, rows, :], preferred_element_type=f32)
    rows = block // nodes
    for z in range(nodes):
        outs[z][...] = jnp.concatenate(
            [total[b * block + z * rows : b * block + (z + 1) * rows] for b in range(n_slices)],
            axis=0,
        ).astype(bf16)


def add_kernel(*refs):
    *parts, out_ref = refs
    total = parts[0][...].astype(f32)
    for part in parts[1:]:
        total += part[...].astype(f32)
    out_ref[...] = total.astype(bf16)


def place_kernel(local, sub, *refs):
    *pieces, out_ref = refs
    me = lax.axis_index("local") * sub + lax.axis_index("sub")
    width = pieces[0].shape[1]
    for r, piece in enumerate(pieces):
        s, x = divmod(r, local)
        at = pl.multiple_of((me ^ (x * sub + s)) * width, LANES)
        out_ref[:, pl.ds(at, width)] = piece[...]


def per_device(tokens, ids, scores, gate_w, up_w, down_w):
    nodes, local, sub = (lax.axis_size(a) for a in ("node", "local", "sub"))
    rows, features = tokens.shape
    local_experts, _, depth = gate_w.shape
    width = down_w.shape[2]
    experts = local_experts * nodes
    n_slices = local * sub
    extra = -(-3 * experts // LANES) * LANES
    block = nodes * rows
    count = n_slices * block

    packed = call(
        functools.partial(pack_kernel, experts),
        jax.ShapeDtypeStruct((rows, features + extra), bf16),
        3,
    )(tokens, ids, scores)
    own = jnp.concatenate([packed] + [swap(packed, "node", z) for z in range(1, nodes)], axis=0)
    blocks = [own] + [swap(own, "local", x) for x in range(1, local)]
    for s in range(1, sub):
        blocks += [swap(b, "sub", s) for b in blocks[:local]]

    hidden = []
    for e in range(local_experts):
        h = call(
            functools.partial(hidden_kernel, e, experts, features),
            jax.ShapeDtypeStruct((count, depth), bf16),
            n_slices + 2,
            flops=4 * count * features * depth,
            size=4 * features * depth,
            vmem=32 if count > 256 else 16,
        )(*blocks, gate_w, up_w)
        parts = [h] + [swap(h, "local", x) for x in range(1, local)]
        for s in range(1, sub):
            parts += [swap(p, "sub", s) for p in parts[:local]]
        hidden += parts

    outs = call(
        functools.partial(down_kernel, local, sub, nodes, local_experts),
        [jax.ShapeDtypeStruct((n_slices * rows, width), bf16)] * nodes,
        len(hidden) + 1,
        flops=2 * count * local_experts * n_slices * depth * width,
        size=2 * local_experts * n_slices * depth * width,
        vmem=32 if count > 256 else 16,
    )(*hidden, down_w)
    arrived = [outs[0]] + [swap(outs[z], "node", z) for z in range(1, nodes)]
    mine = call(
        add_kernel, jax.ShapeDtypeStruct((n_slices * rows, width), bf16), nodes
    )(*arrived)
    pieces = []
    for r in range(n_slices):
        s, x = divmod(r, local)
        piece = mine[r * rows : (r + 1) * rows]
        if r:
            pair = x * sub + s
            piece = lax.ppermute(
                piece, ("local", "sub"), [(i, i ^ pair) for i in range(n_slices)]
            )
        pieces.append(piece)
    if width % LANES == 0:
        return call(
            functools.partial(place_kernel, local, sub),
            jax.ShapeDtypeStruct((rows, features), bf16),
            n_slices,
        )(*pieces)
    me = lax.axis_index("local") * sub + lax.axis_index("sub")
    out = jnp.zeros((rows, features), bf16)
    for r, piece in enumerate(pieces):
        s, x = divmod(r, local)
        out = lax.dynamic_update_slice(out, piece, (0, (me ^ (x * sub + s)) * width))
    return out


def solution(mesh):
    everything = P(("groups", "node", "local", "sub"), None)
    weights = P("node", None, ("local", "sub"))
    return jax.shard_map(
        per_device,
        mesh=mesh,
        in_specs=(everything,) * 3 + (weights,) * 3,
        out_specs=everything,
        check_vma=False,
    )
```

```python
import functools

import jax
import jax.numpy as jnp
from jax import lax
from jax.experimental import pallas as pl
from jax.experimental.pallas import tpu as pltpu
from jax.sharding import PartitionSpec as P

route_scale = 2.827
LANES = 128
f32, bf16 = jnp.float32, jnp.bfloat16
VMEM = pl.BlockSpec(memory_space=pltpu.VMEM)
HBM = pl.BlockSpec(memory_space=pltpu.HBM)


def swap(x, axis, k):
    return lax.ppermute(x, axis, [(i, i ^ k) for i in range(lax.axis_size(axis))])


def in_hbm(x):
    return pltpu.with_memory_space_constraint(x, pltpu.HBM)


def call(kernel, out_shape, n_in, flops=0, size=0, vmem=4, scratch=(), spec=VMEM):
    return pl.pallas_call(
        kernel,
        out_shape=out_shape,
        in_specs=[spec] * n_in,
        out_specs=jax.tree.map(lambda _: VMEM, out_shape),
        scratch_shapes=scratch,
        compiler_params=pltpu.CompilerParams(vmem_limit_bytes=vmem << 20),
        cost_estimate=pl.CostEstimate(flops=flops, bytes_accessed=size, transcendentals=0),
    )


def pack_kernel(experts, tok_hbm, ids_hbm, scores_hbm, out_ref, ids_ref, scores_ref, sems):
    rows, features = tok_hbm.shape
    extra = out_ref.shape[1] - features
    pairs = ((ids_hbm, ids_ref), (scores_hbm, scores_ref), (tok_hbm, out_ref.at[:, :features]))
    copies = [pltpu.make_async_copy(a, b, sems.at[i]) for i, (a, b) in enumerate(pairs)]
    for copy in copies:
        copy.start()
    copies[0].wait()
    copies[1].wait()
    gate = 1.0 / (1.0 + jnp.exp(-scores_ref[...]))
    share = route_scale * gate / jnp.sum(gate, axis=1, keepdims=True)
    column = lax.broadcasted_iota(jnp.int32, (rows, extra), 1)
    expert, term = column % experts, column // experts
    weight = jnp.zeros((rows, extra), f32)
    for k in range(ids_ref.shape[1]):
        weight += jnp.where(ids_ref[:, k : k + 1] == expert, share[:, k : k + 1], 0.0)
    first = weight.astype(bf16).astype(f32)
    second = (weight - first).astype(bf16).astype(f32)
    third = weight - first - second
    terms = jnp.where(term == 0, first, jnp.where(term == 1, second, jnp.where(term == 2, third, 0.0)))
    out_ref[:, features:] = terms.astype(bf16)
    copies[2].wait()


def fetch(parts, after, pieces=4):
    arrays = [p[0] for p in parts]

    def body(*refs):
        n = len(arrays)
        srcs, outs, mark, sems = refs[:n], refs[n + 1 : 2 * n + 1], refs[2 * n + 1], refs[2 * n + 2]
        mark[...] = jnp.zeros_like(mark)
        copies = []
        for (_, first, count), src, out in zip(parts, srcs, outs):
            step = src.shape[1] // pieces
            for e in range(count):
                for p in range(pieces):
                    rows = pl.ds(p * step, step)
                    copies.append(
                        pltpu.make_async_copy(
                            src.at[first + e, rows], out.at[e, rows], sems.at[len(copies)]
                        )
                    )
        for copy in copies:
            copy.start()
        for copy in copies:
            copy.wait()

    shapes = [(count,) + a.shape[1:] for a, _, count in parts]
    return pl.pallas_call(
        body,
        out_shape=[pltpu.VMEM(s, bf16) for s in shapes] + [pltpu.VMEM((8, LANES), f32)],
        in_specs=[HBM] * len(arrays) + [VMEM],
        out_specs=[VMEM] * (len(arrays) + 1),
        scratch_shapes=[pltpu.SemaphoreType.DMA((pieces * sum(s[0] for s in shapes),))],
        compiler_params=pltpu.CompilerParams(vmem_limit_bytes=1 << 20),
        cost_estimate=pl.CostEstimate(
            flops=0, bytes_accessed=sum(2 * s[0] * s[1] * s[2] for s in shapes), transcendentals=0
        ),
    )(*[in_hbm(a) for a in arrays], after)


def stack(parts, after):
    def body(*refs):
        at, out = 0, refs[-1]
        for ref in refs[: len(parts)]:
            rows = ref.shape[0]
            out[at : at + rows, :] = ref[...]
            at += rows

    rows, width = sum(p.shape[0] for p in parts), parts[0].shape[1]
    shape = jax.ShapeDtypeStruct((rows, width), parts[0].dtype)
    return call(body, shape, len(parts) + len(after))(*parts, *after)


def stack_one(part, after):
    def body(ref, _, out):
        out[...] = ref[...]

    return call(body, jax.ShapeDtypeStruct(part.shape, part.dtype), 2)(part, after)


def hidden(blocks, gates, ups, which, experts, features):
    n = len(blocks)
    local_experts, _, depth = ups.shape
    count = sum(b.shape[0] for b in blocks)

    def body(*refs):
        ins, (gate_ref, up_ref, out_ref) = refs[:n], refs[n:]
        x = jnp.concatenate([b[:, :features] for b in ins], axis=0)
        tail = jnp.concatenate([b[:, features:] for b in ins], axis=0).astype(f32)
        column = lax.broadcasted_iota(jnp.int32, tail.shape, 1)
        for i, e in enumerate(which):
            mine = lax.axis_index("node") * local_experts + e
            keep = (column % experts == mine) & (column < 3 * experts)
            weight = jnp.sum(jnp.where(keep, tail, 0.0), axis=1, keepdims=True)
            gate = jnp.dot(x, gate_ref[e], preferred_element_type=f32)
            up = jnp.dot(x, up_ref[e], preferred_element_type=f32)
            out_ref[i] = (gate / (1.0 + jnp.exp(-gate)) * up * weight).astype(bf16)

    shape = jax.ShapeDtypeStruct((len(which), count, depth), bf16)
    work = len(which) * features * depth
    return call(
        body, shape, n + 2, 4 * count * work, 4 * work, 32 if count > 128 else 4
    )(*blocks, gates, ups)


def down(terms, total, weights, local, sub, nodes, last):
    n_slices = local * sub
    arrays = []
    for term in terms:
        if not any(term[0] is a for a in arrays):
            arrays.append(term[0])
    index = [next(i for i, a in enumerate(arrays) if a is term[0]) for term in terms]
    tokens, width = total
    block = tokens // n_slices
    depth = terms[0][0].shape[2]
    rows = block // nodes
    before = [] if last is None else [last]

    def place(r):
        s, x = divmod(r, local)
        return (lax.axis_index("local") * sub + lax.axis_index("sub")) ^ (x * sub + s)

    def body(*refs):
        ins = refs[: len(arrays)]
        down_ref, out_ref = refs[len(arrays)], refs[-1]
        acc = [None] * n_slices
        if before:
            for b in range(n_slices):
                acc[b] = refs[len(arrays) + 1][b * block : (b + 1) * block, :]
        groups = {}
        for i, (_, entry, e, r, blocks) in zip(index, terms):
            groups.setdefault((e, r), []).append((i, entry, blocks))
        for (e, r), members in groups.items():
            w = down_ref[e, pl.ds(pl.multiple_of(place(r) * depth, depth), depth), :]
            h = jnp.concatenate([ins[i][entry] for i, entry, _ in members], axis=0)
            product = jnp.dot(h, w, preferred_element_type=f32)
            for j, b in enumerate(b for m in members for b in m[2]):
                part = product[j * block : (j + 1) * block]
                acc[b] = part if acc[b] is None else acc[b] + part
        if not before:
            for b in range(n_slices):
                out_ref[b * block : (b + 1) * block, :] = acc[b]
            return
        node = lax.axis_index("node")
        for b in range(n_slices):
            for z in range(nodes):
                out_ref[(node ^ z) * n_slices + place(b)] = acc[b][z * rows : (z + 1) * rows].astype(
                    bf16
                )

    shape = (
        jax.ShapeDtypeStruct((nodes * n_slices, rows, width), bf16)
        if before
        else jax.ShapeDtypeStruct((tokens, width), f32)
    )
    pairs = {(t[2], t[3]) for t in terms}
    return call(
        body,
        shape,
        len(arrays) + 1 + len(before),
        2 * tokens * len(pairs) * depth * width,
        2 * len(pairs) * depth * width,
        32 if tokens > 256 else 4,
    )(*arrays, weights, *before)


def sum_kernel(nodes, in_ref, out_ref):
    n_slices, width = in_ref.shape[0] // nodes, in_ref.shape[2]
    for i in range(n_slices):
        total = in_ref[i].astype(f32)
        for n in range(1, nodes):
            total += in_ref[n * n_slices + i].astype(f32)
        out_ref[:, i * width : (i + 1) * width] = total.astype(bf16)


def per_device(tokens, ids, scores, gate_w, up_w, down_w):
    nodes, local, sub = (lax.axis_size(a) for a in ("node", "local", "sub"))
    rows, features = tokens.shape
    local_experts, _, depth = gate_w.shape
    width = down_w.shape[2]
    experts = local_experts * nodes
    n_slices = local * sub
    extra = -(-3 * experts // LANES) * LANES
    count = n_slices * nodes * rows

    packed = call(
        functools.partial(pack_kernel, experts),
        jax.ShapeDtypeStruct((rows, features + extra), bf16),
        3,
        scratch=[
            pltpu.VMEM(ids.shape, ids.dtype),
            pltpu.VMEM(scores.shape, f32),
            pltpu.SemaphoreType.DMA((3,)),
        ],
        spec=HBM,
    )(in_hbm(tokens), in_hbm(ids), in_hbm(scores))
    early = [swap(packed, "local", x) for x in range(1, local)]
    others = [swap(packed, "node", z) for z in range(1, nodes)]
    gates, mark = fetch([(gate_w, 0, local_experts)], packed)
    rest = stack(others, [mark] + early)
    far = [swap(rest, "local", x) for x in range(1, local)]
    ups, mark = fetch([(up_w, 0, local_experts)], rest)

    blocks = [stack([packed, rest], [])]
    blocks += [stack(pair, [mark]) for pair in zip(early, far)]
    for s in range(1, sub):
        blocks += [swap(b, "sub", s) for b in blocks[:local]]

    def spread(parts, e, over):
        terms = []
        for x, part in enumerate(parts):
            for s in over:
                r = s * local + x
                piece = swap(part, "sub", s) if s else part
                terms.append((piece, 0, e, r, [b ^ r for b in range(n_slices)]))
        return terms

    soon, late = [], []
    for e in range(local_experts):
        h = hidden(blocks, gates, ups, [e], experts, features)
        parts = [h] + [swap(h, "local", x) for x in range(1, local)]
        if e < local_experts - 1:
            terms = spread(parts, e, range(sub))
            soon += [t for t in terms if t[3] <= local]
            late += [t for t in terms if t[3] > local]
    soon += spread(parts[:1], e, range(sub))
    shape = (count, width)
    total = down(soon, shape, down_w, local, sub, nodes, None)
    parts[1:] = [stack_one(p, total) for p in parts[1:]]
    late += [t for t in spread(parts, e, range(sub)) if t[3] % local]
    part = down(late, shape, down_w, local, sub, nodes, total)
    part = lax.all_to_all(part, ("node", "local", "sub"), 0, 0, tiled=True)
    return call(
        functools.partial(sum_kernel, nodes), jax.ShapeDtypeStruct((rows, features), bf16), 1
    )(part)


def solution(mesh):
    everything = P(("groups", "node", "local", "sub"), None)
    weights = P("node", None, ("local", "sub"))
    return jax.shard_map(
        per_device,
        mesh=mesh,
        in_specs=(everything,) * 3 + (weights,) * 3,
        out_specs=everything,
        check_vma=False,
    )
```

```python
import functools

import jax
import jax.numpy as jnp
from jax import lax
from jax.experimental import pallas as pl
from jax.experimental.pallas import tpu as pltpu
from jax.sharding import PartitionSpec as P

route_scale = 2.827
LANES = 128
f32, bf16 = jnp.float32, jnp.bfloat16
VMEM = pl.BlockSpec(memory_space=pltpu.VMEM)
HBM = pl.BlockSpec(memory_space=pltpu.HBM)


def swap(x, **by):
    axes = tuple(by)
    sizes = [lax.axis_size(a) for a in axes]
    pairs = []
    for i in range(functools.reduce(lambda a, b: a * b, sizes)):
        rest, at, to, stride = i, [], 0, 1
        for size, k in zip(sizes[::-1], list(by.values())[::-1]):
            to += ((rest % size) ^ k) * stride
            stride *= size
            rest //= size
        pairs.append((i, to))
    return lax.ppermute(x, axes if len(axes) > 1 else axes[0], pairs)


def in_hbm(x):
    return pltpu.with_memory_space_constraint(x, pltpu.HBM)


def call(kernel, out_shape, args, beside=(), scratch=(), spec=VMEM, flops=0, size=0, vmem=4):
    n = len(args)

    def body(*refs):
        kernel(*refs[:n], *refs[n + len(beside) :])

    return pl.pallas_call(
        body,
        out_shape=out_shape,
        in_specs=[spec] * n + [HBM] * len(beside),
        out_specs=jax.tree.map(lambda _: VMEM, out_shape),
        scratch_shapes=scratch,
        compiler_params=pltpu.CompilerParams(vmem_limit_bytes=vmem << 20),
        cost_estimate=pl.CostEstimate(flops=flops, bytes_accessed=size, transcendentals=0)
        if size
        else None,
    )(*args, *[in_hbm(b) for b in beside])


def pack_kernel(experts, tok_hbm, ids_hbm, scores_hbm, out_ref, ids_ref, scores_ref, sems):
    rows, features = tok_hbm.shape
    extra = out_ref.shape[1] - features
    pairs = ((ids_hbm, ids_ref), (scores_hbm, scores_ref), (tok_hbm, out_ref.at[:, :features]))
    copies = [pltpu.make_async_copy(a, b, sems.at[i]) for i, (a, b) in enumerate(pairs)]
    for copy in copies:
        copy.start()
    copies[0].wait()
    copies[1].wait()
    gate = 1.0 / (1.0 + jnp.exp(-scores_ref[...]))
    share = route_scale * gate / jnp.sum(gate, axis=1, keepdims=True)
    column = lax.broadcasted_iota(jnp.int32, (rows, extra), 1)
    expert, term = column % experts, column // experts
    weight = jnp.zeros((rows, extra), f32)
    for k in range(ids_ref.shape[1]):
        weight += jnp.where(ids_ref[:, k : k + 1] == expert, share[:, k : k + 1], 0.0)
    first = weight.astype(bf16).astype(f32)
    second = (weight - first).astype(bf16).astype(f32)
    third = weight - first - second
    terms = jnp.where(term == 0, first, jnp.where(term == 1, second, jnp.where(term == 2, third, 0.0)))
    out_ref[:, features:] = terms.astype(bf16)
    copies[2].wait()


def stack(parts, after=(), beside=(), order=None, cuts=((0, None),)):
    operands = [*parts, *after]
    order = list(range(len(operands))) if order is None else order
    spans = [parts[first:end] for first, end in cuts]

    def kernel(*refs):
        for (first, _), span, out in zip(cuts, spans, refs[len(operands) :]):
            at = 0
            for i in range(first, first + len(span)):
                ref = refs[order.index(i)]
                rows = ref.shape[0]
                out[at : at + rows, :] = ref[...]
                at += rows

    width, kind = parts[0].shape[1], parts[0].dtype
    shapes = [jax.ShapeDtypeStruct((sum(p.shape[0] for p in span), width), kind) for span in spans]
    out = call(kernel, shapes, [operands[i] for i in order], beside)
    return out if len(cuts) > 1 else out[0]


def hidden(blocks, gate_w, up_w, e, features):
    n = len(blocks)
    local_experts, _, depth = gate_w.shape
    count = sum(b.shape[0] for b in blocks)

    def kernel(*refs):
        *ins, gate_ref, up_ref, out_ref = refs
        experts = local_experts * lax.axis_size("node")
        x = jnp.concatenate([b[:, :features] for b in ins], axis=0)
        tail = jnp.concatenate([b[:, features:] for b in ins], axis=0).astype(f32)
        column = lax.broadcasted_iota(jnp.int32, tail.shape, 1)
        mine = lax.axis_index("node") * local_experts + e
        keep = (column % experts == mine) & (column < 3 * experts)
        weight = jnp.sum(jnp.where(keep, tail, 0.0), axis=1, keepdims=True)
        gate = jnp.dot(x, gate_ref[e], preferred_element_type=f32)
        up = jnp.dot(x, up_ref[e], preferred_element_type=f32)
        out_ref[...] = (gate / (1.0 + jnp.exp(-gate)) * up * weight).astype(bf16)

    return call(
        kernel,
        jax.ShapeDtypeStruct((count, depth), bf16),
        [*blocks, gate_w, up_w],
        flops=4 * count * features * depth,
        size=4 * features * depth,
        vmem=32 if count > 128 else 4,
    )


def down(terms, weights, last, local, sub, nodes, final):
    n_slices = local * sub
    arrays = []
    for term in terms:
        if not any(term[0] is a for a in arrays):
            arrays.append(term[0])
    index = [next(i for i, a in enumerate(arrays) if a is term[0]) for term in terms]
    depth = weights.shape[1] // n_slices
    width = weights.shape[2]
    tokens = terms[0][4]
    block = tokens // n_slices
    rows = block // nodes
    before = [] if last is None else [last]

    def kernel(*refs):
        ins, down_ref = refs[: len(arrays)], refs[len(arrays)]
        outs = refs[len(arrays) + 1 + len(before) :]
        me = lax.axis_index("local") * sub + lax.axis_index("sub")
        total = refs[len(arrays) + 1][...] if before else None
        for i, (_, at, e, r, _) in zip(index, terms):
            s, x = divmod(r, local)
            here = pl.ds(pl.multiple_of((me ^ (x * sub + s)) * depth, depth), depth)
            h = [ins[i][pl.ds(at + (b ^ r) * block, block), :] for b in range(n_slices)]
            product = jnp.dot(
                jnp.concatenate(h, axis=0), down_ref[e, here, :], preferred_element_type=f32
            )
            total = product if total is None else total + product
        if not final:
            outs[0][...] = total
            return
        for z in range(nodes):
            starts = [b * block + z * rows for b in range(n_slices)]
            outs[z][...] = jnp.concatenate([total[a : a + rows] for a in starts], axis=0).astype(bf16)

    shape = (
        [jax.ShapeDtypeStruct((n_slices * rows, width), bf16)] * nodes
        if final
        else jax.ShapeDtypeStruct((tokens, width), f32)
    )
    return call(
        kernel,
        shape,
        [*arrays, weights, *before],
        flops=2 * len(terms) * tokens * depth * width,
        size=2 * len(terms) * depth * width,
        vmem=32 if tokens > 256 else 4,
    )


def add_up(parts, rows, n_slices):
    def kernel(*refs):
        ins, outs = refs[: len(parts)], refs[len(parts) :]
        total = ins[0][...].astype(f32)
        for ref in ins[1:]:
            total += ref[...].astype(f32)
        for r, out in enumerate(outs):
            out[...] = total[r * rows : (r + 1) * rows].astype(bf16)

    shape = jax.ShapeDtypeStruct((rows, parts[0].shape[1]), bf16)
    return call(kernel, [shape] * n_slices, parts)


def place_kernel(local, sub, *refs):
    *pieces, out_ref = refs
    me = lax.axis_index("local") * sub + lax.axis_index("sub")
    width = pieces[0].shape[1]
    for r, piece in enumerate(pieces):
        s, x = divmod(r, local)
        at = pl.multiple_of((me ^ (x * sub + s)) * width, LANES)
        out_ref[:, pl.ds(at, width)] = piece[...]


def per_device(tokens, ids, scores, gate_w, up_w, down_w):
    nodes, local, sub = (lax.axis_size(a) for a in ("node", "local", "sub"))
    rows, features = tokens.shape
    local_experts, _, depth = gate_w.shape
    width = down_w.shape[2]
    experts = local_experts * nodes
    n_slices = local * sub
    extra = -(-3 * experts // LANES) * LANES
    count = n_slices * nodes * rows

    packed = call(
        functools.partial(pack_kernel, experts),
        jax.ShapeDtypeStruct((rows, features + extra), bf16),
        [in_hbm(tokens), in_hbm(ids), in_hbm(scores)],
        scratch=[
            pltpu.VMEM(ids.shape, ids.dtype),
            pltpu.VMEM(scores.shape, f32),
            pltpu.SemaphoreType.DMA((3,)),
        ],
        spec=HBM,
    )
    direct = min(1, nodes)
    over = [[packed] + [swap(packed, node=z) for z in range(1, nodes)]]
    for x in range(1, local):
        over.append([swap(packed, local=x)])
        over[x] += [swap(packed, node=z, local=x) for z in range(1, direct)]
    early = [b for x in range(1, local) for b in over[x]]
    own, rest = stack(over[0], early, (gate_w, up_w), [4, 1, 3, 2, 0] if nodes == 4 else None, ((0, None), (direct, None)))
    far = [swap(rest, local=x) for x in range(1, local)]

    blocks = [own]
    blocks += [stack(over[x] + [far[x - 1]], (), (gate_w,)) for x in range(1, local)]
    for s in range(1, sub):
        blocks += [swap(b, sub=s) for b in blocks[:local]]

    units, crossed = [], []
    for e in range(local_experts):
        h = hidden(blocks, gate_w, up_w, e, features)
        units.append(h)
        crossed.append([swap(h, local=x) for x in range(1, local)])
    e = local_experts - 1

    def terms_of(array, at, e, r):
        return [(array, at, e, r, count)]

    add = functools.partial(down, weights=down_w, local=local, sub=sub, nodes=nodes)
    parts = [(units[e], e, 0) for e in range(local_experts)]
    parts += [(c, e, x + 1) for e in range(local_experts - 1) for x, c in enumerate(crossed[e])]
    terms = [(array, 0, e, x, count) for array, e, x in parts]
    total = add(terms, last=None, final=False)
    terms = []
    for s in range(1, sub):
        for array, e, x in parts:
            terms.append((swap(array, sub=s), 0, e, s * local + x, count))
    e = local_experts - 1
    joined = stack(crossed[e], [total]) if local > 1 else None
    terms += [(joined, (x - 1) * count, e, x, count) for x in range(1, local)]
    if terms:
        total = add(terms, last=total, final=False)
    terms = []
    for s in range(1, sub):
        got = swap(joined, sub=s)
        terms += [(got, (x - 1) * count, e, s * local + x, count) for x in range(1, local)]
    sent = add(terms, last=total, final=True)

    arrived = [sent[0]] + [swap(sent[z], node=z) for z in range(1, nodes)]
    order = list(range(nodes))[::-1]
    pieces = list(add_up([arrived[z] for z in order], rows, n_slices))
    for r in range(1, n_slices):
        s, x = divmod(r, local)
        by = {a: k for a, k in (("local", x), ("sub", s)) if k}
        pieces[r] = swap(pieces[r], **by)
    if width % LANES == 0:
        shape = jax.ShapeDtypeStruct((rows, features), bf16)
        return call(functools.partial(place_kernel, local, sub), shape, pieces)
    me = lax.axis_index("local") * sub + lax.axis_index("sub")
    out = jnp.zeros((rows, features), bf16)
    for r, piece in enumerate(pieces):
        s, x = divmod(r, local)
        out = lax.dynamic_update_slice(out, piece, (0, (me ^ (x * sub + s)) * width))
    return out


def solution(mesh):
    everything = P(("groups", "node", "local", "sub"), None)
    weights = P("node", None, ("local", "sub"))
    return jax.shard_map(
        per_device,
        mesh=mesh,
        in_specs=(everything,) * 3 + (weights,) * 3,
        out_specs=everything,
        check_vma=False,
    )
```

```python
import functools

import jax
import jax.numpy as jnp
from jax import lax
from jax.experimental import pallas as pl
from jax.experimental.pallas import tpu as pltpu
from jax.sharding import PartitionSpec as P

route_scale = 2.827
LANES = 128
f32, bf16 = jnp.float32, jnp.bfloat16
VMEM = pl.BlockSpec(memory_space=pltpu.VMEM)
HBM = pl.BlockSpec(memory_space=pltpu.HBM)


def swap(x, **by):
    axes = tuple(by)
    sizes = [lax.axis_size(a) for a in axes]
    pairs = []
    for i in range(functools.reduce(lambda a, b: a * b, sizes)):
        rest, at, to, stride = i, [], 0, 1
        for size, k in zip(sizes[::-1], list(by.values())[::-1]):
            to += ((rest % size) ^ k) * stride
            stride *= size
            rest //= size
        pairs.append((i, to))
    return lax.ppermute(x, axes if len(axes) > 1 else axes[0], pairs)


def in_hbm(x):
    return pltpu.with_memory_space_constraint(x, pltpu.HBM)


def call(kernel, out_shape, args, beside=(), scratch=(), spec=VMEM, flops=0, size=0, vmem=4):
    n = len(args)

    def body(*refs):
        kernel(*refs[:n], *refs[n + len(beside) :])

    return pl.pallas_call(
        body,
        out_shape=out_shape,
        in_specs=[spec] * n + [HBM] * len(beside),
        out_specs=jax.tree.map(lambda _: VMEM, out_shape),
        scratch_shapes=scratch,
        compiler_params=pltpu.CompilerParams(vmem_limit_bytes=vmem << 20),
        cost_estimate=pl.CostEstimate(flops=flops, bytes_accessed=size, transcendentals=0)
        if size
        else None,
    )(*args, *[in_hbm(b) for b in beside])


def pack_kernel(experts, tok_hbm, ids_hbm, scores_hbm, out_ref, ids_ref, scores_ref, sems):
    rows, features = tok_hbm.shape
    extra = out_ref.shape[1] - features
    pairs = ((ids_hbm, ids_ref), (scores_hbm, scores_ref), (tok_hbm, out_ref.at[:, :features]))
    copies = [pltpu.make_async_copy(a, b, sems.at[i]) for i, (a, b) in enumerate(pairs)]
    for copy in copies:
        copy.start()
    copies[0].wait()
    copies[1].wait()
    gate = 1.0 / (1.0 + jnp.exp(-scores_ref[...]))
    share = route_scale * gate / jnp.sum(gate, axis=1, keepdims=True)
    column = lax.broadcasted_iota(jnp.int32, (rows, extra), 1)
    expert, term = column % experts, column // experts
    weight = jnp.zeros((rows, extra), f32)
    for k in range(ids_ref.shape[1]):
        weight += jnp.where(ids_ref[:, k : k + 1] == expert, share[:, k : k + 1], 0.0)
    first = weight.astype(bf16).astype(f32)
    second = (weight - first).astype(bf16).astype(f32)
    third = weight - first - second
    terms = jnp.where(term == 0, first, jnp.where(term == 1, second, jnp.where(term == 2, third, 0.0)))
    out_ref[:, features:] = terms.astype(bf16)
    copies[2].wait()


def stack(parts, after=(), beside=(), order=None, cuts=((0, None),)):
    operands = [*parts, *after]
    order = list(range(len(operands))) if order is None else order
    spans = [parts[first:end] for first, end in cuts]

    def kernel(*refs):
        for (first, _), span, out in zip(cuts, spans, refs[len(operands) :]):
            at = 0
            for i in range(first, first + len(span)):
                ref = refs[order.index(i)]
                rows = ref.shape[0]
                out[at : at + rows, :] = ref[...]
                at += rows

    width, kind = parts[0].shape[1], parts[0].dtype
    shapes = [jax.ShapeDtypeStruct((sum(p.shape[0] for p in span), width), kind) for span in spans]
    out = call(kernel, shapes, [operands[i] for i in order], beside)
    return out if len(cuts) > 1 else out[0]


def hidden(blocks, gate_w, up_w, e, features):
    n = len(blocks)
    local_experts, _, depth = gate_w.shape
    count = sum(b.shape[0] for b in blocks)

    def kernel(*refs):
        *ins, gate_ref, up_ref, out_ref = refs
        experts = local_experts * lax.axis_size("node")
        x = jnp.concatenate([b[:, :features] for b in ins], axis=0)
        tail = jnp.concatenate([b[:, features:] for b in ins], axis=0).astype(f32)
        column = lax.broadcasted_iota(jnp.int32, tail.shape, 1)
        mine = lax.axis_index("node") * local_experts + e
        keep = (column % experts == mine) & (column < 3 * experts)
        weight = jnp.sum(jnp.where(keep, tail, 0.0), axis=1, keepdims=True)
        gate = jnp.dot(x, gate_ref[e], preferred_element_type=f32)
        up = jnp.dot(x, up_ref[e], preferred_element_type=f32)
        out_ref[...] = (gate / (1.0 + jnp.exp(-gate)) * up * weight).astype(bf16)

    return call(
        kernel,
        jax.ShapeDtypeStruct((count, depth), bf16),
        [*blocks, gate_w, up_w],
        flops=4 * count * features * depth,
        size=4 * features * depth,
        vmem=32 if count > 128 else 4,
    )


def down(terms, weights, last, local, sub, nodes, final):
    n_slices = local * sub
    arrays = []
    for term in terms:
        if not any(term[0] is a for a in arrays):
            arrays.append(term[0])
    index = [next(i for i, a in enumerate(arrays) if a is term[0]) for term in terms]
    depth = weights.shape[1] // n_slices
    width = weights.shape[2]
    tokens = terms[0][4]
    block = tokens // n_slices
    rows = block // nodes
    before = [] if last is None else [last]

    def kernel(*refs):
        ins, down_ref = refs[: len(arrays)], refs[len(arrays)]
        outs = refs[len(arrays) + 1 + len(before) :]
        me = lax.axis_index("local") * sub + lax.axis_index("sub")
        total = refs[len(arrays) + 1][...] if before else None
        for i, (_, at, e, r, _) in zip(index, terms):
            s, x = divmod(r, local)
            here = pl.ds(pl.multiple_of((me ^ (x * sub + s)) * depth, depth), depth)
            h = [ins[i][pl.ds(at + (b ^ r) * block, block), :] for b in range(n_slices)]
            product = jnp.dot(
                jnp.concatenate(h, axis=0), down_ref[e, here, :], preferred_element_type=f32
            )
            total = product if total is None else total + product
        if not final:
            outs[0][...] = total
            return
        for z in range(nodes):
            starts = [b * block + z * rows for b in range(n_slices)]
            outs[z][...] = jnp.concatenate([total[a : a + rows] for a in starts], axis=0).astype(bf16)

    shape = (
        [jax.ShapeDtypeStruct((n_slices * rows, width), bf16)] * nodes
        if final
        else jax.ShapeDtypeStruct((tokens, width), f32)
    )
    return call(
        kernel,
        shape,
        [*arrays, weights, *before],
        flops=2 * len(terms) * tokens * depth * width,
        size=2 * len(terms) * depth * width,
        vmem=32 if tokens > 256 else 4,
    )


def add_up(parts, rows, n_slices):
    def kernel(*refs):
        ins, outs = refs[: len(parts)], refs[len(parts) :]
        total = ins[0][...].astype(f32)
        for ref in ins[1:]:
            total += ref[...].astype(f32)
        for r, out in enumerate(outs):
            out[...] = total[r * rows : (r + 1) * rows].astype(bf16)

    shape = jax.ShapeDtypeStruct((rows, parts[0].shape[1]), bf16)
    return call(kernel, [shape] * n_slices, parts)


def place_kernel(local, sub, order, *refs):
    *pieces, out_ref = refs
    me = lax.axis_index("local") * sub + lax.axis_index("sub")
    width = pieces[0].shape[1]
    for r, piece in zip(order, pieces):
        s, x = divmod(r, local)
        at = pl.multiple_of((me ^ (x * sub + s)) * width, LANES)
        out_ref[:, pl.ds(at, width)] = piece[...]


def per_device(tokens, ids, scores, gate_w, up_w, down_w):
    nodes, local, sub = (lax.axis_size(a) for a in ("node", "local", "sub"))
    rows, features = tokens.shape
    local_experts, _, depth = gate_w.shape
    width = down_w.shape[2]
    experts = local_experts * nodes
    n_slices = local * sub
    extra = -(-3 * experts // LANES) * LANES
    count = n_slices * nodes * rows

    packed = call(
        functools.partial(pack_kernel, experts),
        jax.ShapeDtypeStruct((rows, features + extra), bf16),
        [in_hbm(tokens), in_hbm(ids), in_hbm(scores)],
        scratch=[
            pltpu.VMEM(ids.shape, ids.dtype),
            pltpu.VMEM(scores.shape, f32),
            pltpu.SemaphoreType.DMA((3,)),
        ],
        spec=HBM,
    )
    direct = min(1, nodes)
    over = [[packed] + [swap(packed, node=z) for z in range(1, nodes)]]
    for x in range(1, local):
        over.append([swap(packed, local=x)])
        over[x] += [swap(packed, node=z, local=x) for z in range(1, direct)]
    early = [b for x in range(1, local) for b in over[x]]
    own, rest = stack(over[0], early, (gate_w, up_w), [4,1,3,2,0] if nodes == 4 else None, ((0, None), (direct, None)))
    far = [swap(rest, local=x) for x in range(1, local)]

    blocks = [own]
    blocks += [stack(over[x] + [far[x - 1]], (), (gate_w,)) for x in range(1, local)]
    for s in range(1, sub):
        blocks += [swap(b, sub=s) for b in blocks[:local]]

    units, crossed = [], []
    for e in range(local_experts):
        h = hidden(blocks, gate_w, up_w, e, features)
        units.append(h)
        crossed.append([swap(h, local=x) for x in range(1, local)])
    e = local_experts - 1

    def terms_of(array, at, e, r):
        return [(array, at, e, r, count)]

    add = functools.partial(down, weights=down_w, local=local, sub=sub, nodes=nodes)
    parts = [(units[e], e, 0) for e in range(local_experts)]
    parts += [(c, e, x + 1) for e in range(local_experts - 1) for x, c in enumerate(crossed[e])]
    terms = [(array, 0, e, x, count) for array, e, x in parts]
    total = add(terms, last=None, final=False)
    terms = []
    for s in range(1, sub):
        for array, e, x in parts:
            terms.append((swap(array, sub=s), 0, e, s * local + x, count))
    e = local_experts - 1
    joined = stack(crossed[e], [total]) if local > 1 else None
    terms += [(joined, (x - 1) * count, e, x, count) for x in range(1, local)]
    if terms:
        total = add(terms, last=total, final=False)
    terms = []
    for s in range(1, sub):
        got = swap(joined, sub=s)
        terms += [(got, (x - 1) * count, e, s * local + x, count) for x in range(1, local)]
    sent = add(terms, last=total, final=True)

    arrived = [sent[0]] + [swap(sent[z], node=z) for z in range(1, nodes)]
    order = [3,1,2,0] if nodes == 4 else list(range(nodes))
    pieces = list(add_up([arrived[z] for z in order], rows, n_slices))
    for r in range(1, n_slices):
        s, x = divmod(r, local)
        by = {a: k for a, k in (("local", x), ("sub", s)) if k}
        pieces[r] = swap(pieces[r], **by)
    if width % LANES == 0:
        shape = jax.ShapeDtypeStruct((rows, features), bf16)
        order = [0, 3, 1, 2] if n_slices == 4 else list(range(n_slices))
        return call(functools.partial(place_kernel, local, sub, order), shape, [pieces[r] for r in order])
    me = lax.axis_index("local") * sub + lax.axis_index("sub")
    out = jnp.zeros((rows, features), bf16)
    for r, piece in enumerate(pieces):
        s, x = divmod(r, local)
        out = lax.dynamic_update_slice(out, piece, (0, (me ^ (x * sub + s)) * width))
    return out


def solution(mesh):
    everything = P(("groups", "node", "local", "sub"), None)
    weights = P("node", None, ("local", "sub"))
    return jax.shard_map(
        per_device,
        mesh=mesh,
        in_specs=(everything,) * 3 + (weights,) * 3,
        out_specs=everything,
        check_vma=False,
    )
```

```python
import functools

import jax
import jax.numpy as jnp
from jax import lax
from jax.experimental import pallas as pl
from jax.experimental.pallas import tpu as pltpu
from jax.sharding import PartitionSpec as P

route_scale = 2.827
LANES = 128
f32, bf16 = jnp.float32, jnp.bfloat16
VMEM = pl.BlockSpec(memory_space=pltpu.VMEM)
HBM = pl.BlockSpec(memory_space=pltpu.HBM)


def swap(x, **by):
    axes = tuple(by)
    sizes = [lax.axis_size(a) for a in axes]
    pairs = []
    for i in range(functools.reduce(lambda a, b: a * b, sizes)):
        rest, at, to, stride = i, [], 0, 1
        for size, k in zip(sizes[::-1], list(by.values())[::-1]):
            to += ((rest % size) ^ k) * stride
            stride *= size
            rest //= size
        pairs.append((i, to))
    return lax.ppermute(x, axes if len(axes) > 1 else axes[0], pairs)


def in_hbm(x):
    return pltpu.with_memory_space_constraint(x, pltpu.HBM)


def call(kernel, out_shape, args, beside=(), scratch=(), spec=VMEM, flops=0, size=0, vmem=4):
    n = len(args)

    def body(*refs):
        kernel(*refs[:n], *refs[n + len(beside) :])

    return pl.pallas_call(
        body,
        out_shape=out_shape,
        in_specs=[spec] * n + [HBM] * len(beside),
        out_specs=jax.tree.map(lambda _: VMEM, out_shape),
        scratch_shapes=scratch,
        compiler_params=pltpu.CompilerParams(vmem_limit_bytes=vmem << 20),
        cost_estimate=pl.CostEstimate(flops=flops, bytes_accessed=size, transcendentals=0)
        if size
        else None,
    )(*args, *[in_hbm(b) for b in beside])


def pack_kernel(experts, tok_hbm, ids_hbm, scores_hbm, out_ref, ids_ref, scores_ref, sems):
    rows, features = tok_hbm.shape
    extra = out_ref.shape[1] - features
    pairs = ((ids_hbm, ids_ref), (scores_hbm, scores_ref), (tok_hbm, out_ref.at[:, :features]))
    copies = [pltpu.make_async_copy(a, b, sems.at[i]) for i, (a, b) in enumerate(pairs)]
    for copy in copies:
        copy.start()
    copies[0].wait()
    copies[1].wait()
    gate = 1.0 / (1.0 + jnp.exp(-scores_ref[...]))
    share = route_scale * gate / jnp.sum(gate, axis=1, keepdims=True)
    column = lax.broadcasted_iota(jnp.int32, (rows, extra), 1)
    expert, term = column % experts, column // experts
    weight = jnp.zeros((rows, extra), f32)
    for k in range(ids_ref.shape[1]):
        weight += jnp.where(ids_ref[:, k : k + 1] == expert, share[:, k : k + 1], 0.0)
    first = weight.astype(bf16).astype(f32)
    second = (weight - first).astype(bf16).astype(f32)
    third = weight - first - second
    terms = jnp.where(term == 0, first, jnp.where(term == 1, second, jnp.where(term == 2, third, 0.0)))
    out_ref[:, features:] = terms.astype(bf16)
    copies[2].wait()


def stack(parts, after=(), beside=(), order=None, cuts=((0, None),)):
    operands = [*parts, *after]
    order = list(range(len(operands))) if order is None else order
    spans = [parts[first:end] for first, end in cuts]

    def kernel(*refs):
        for (first, _), span, out in zip(cuts, spans, refs[len(operands) :]):
            at = 0
            for i in range(first, first + len(span)):
                ref = refs[order.index(i)]
                rows = ref.shape[0]
                out[at : at + rows, :] = ref[...]
                at += rows

    width, kind = parts[0].shape[1], parts[0].dtype
    shapes = [jax.ShapeDtypeStruct((sum(p.shape[0] for p in span), width), kind) for span in spans]
    out = call(kernel, shapes, [operands[i] for i in order], beside)
    return out if len(cuts) > 1 else out[0]


def hidden(blocks, gate_w, up_w, e, features):
    n = len(blocks)
    local_experts, _, depth = gate_w.shape
    count = sum(b.shape[0] for b in blocks)

    def kernel(*refs):
        *ins, gate_ref, up_ref, out_ref = refs
        experts = local_experts * lax.axis_size("node")
        x = jnp.concatenate([b[:, :features] for b in ins], axis=0)
        tail = jnp.concatenate([b[:, features:] for b in ins], axis=0).astype(f32)
        column = lax.broadcasted_iota(jnp.int32, tail.shape, 1)
        mine = lax.axis_index("node") * local_experts + e
        keep = (column % experts == mine) & (column < 3 * experts)
        weight = jnp.sum(jnp.where(keep, tail, 0.0), axis=1, keepdims=True)
        gate = jnp.dot(x, gate_ref[e], preferred_element_type=f32)
        up = jnp.dot(x, up_ref[e], preferred_element_type=f32)
        out_ref[...] = (gate / (1.0 + jnp.exp(-gate)) * up * weight).astype(bf16)

    return call(
        kernel,
        jax.ShapeDtypeStruct((count, depth), bf16),
        [*blocks, gate_w, up_w],
        flops=4 * count * features * depth,
        size=4 * features * depth,
        vmem=32 if count > 128 else 4,
    )


def down(terms, weights, last, tokens, local, sub, nodes, final):
    n_slices = local * sub
    arrays = []
    for term in terms:
        if not any(term[0] is a for a in arrays):
            arrays.append(term[0])
    index = [next(i for i, a in enumerate(arrays) if a is term[0]) for term in terms]
    depth = weights.shape[1] // n_slices
    width = weights.shape[2]
    block = tokens // n_slices
    rows = block // nodes
    before = [] if last is None else [last]

    def kernel(*refs):
        ins, down_ref = refs[: len(arrays)], refs[len(arrays)]
        outs = refs[len(arrays) + 1 + len(before) :]
        me = lax.axis_index("local") * sub + lax.axis_index("sub")
        total = refs[len(arrays) + 1][...] if before else None
        for i, (_, at, e, r) in zip(index, terms):
            s, x = divmod(r, local)
            here = pl.ds(pl.multiple_of((me ^ (x * sub + s)) * depth, depth), depth)
            h = [ins[i][pl.ds(at + (b ^ r) * block, block), :] for b in range(n_slices)]
            product = jnp.dot(
                jnp.concatenate(h, axis=0), down_ref[e, here, :], preferred_element_type=f32
            )
            total = product if total is None else total + product
        if not final:
            outs[0][...] = total
            return
        for z in range(nodes):
            starts = [b * block + z * rows for b in range(n_slices)]
            outs[z][...] = jnp.concatenate([total[a : a + rows] for a in starts], axis=0).astype(bf16)

    shape = (
        [jax.ShapeDtypeStruct((n_slices * rows, width), bf16)] * nodes
        if final
        else jax.ShapeDtypeStruct((tokens, width), f32)
    )
    return call(
        kernel,
        shape,
        [*arrays, weights, *before],
        flops=2 * len(terms) * tokens * depth * width,
        size=2 * len(terms) * depth * width,
        vmem=32 if tokens > 256 else 4,
    )


def add_up(parts, rows, n_slices):
    def kernel(*refs):
        ins, outs = refs[: len(parts)], refs[len(parts) :]
        total = ins[0][...].astype(f32)
        for ref in ins[1:]:
            total += ref[...].astype(f32)
        for r, out in enumerate(outs):
            out[...] = total[r * rows : (r + 1) * rows].astype(bf16)

    shape = jax.ShapeDtypeStruct((rows, parts[0].shape[1]), bf16)
    return call(kernel, [shape] * n_slices, parts)


def place_kernel(local, sub, order, *refs):
    *pieces, out_ref = refs
    me = lax.axis_index("local") * sub + lax.axis_index("sub")
    width = pieces[0].shape[1]
    for r, piece in zip(order, pieces):
        s, x = divmod(r, local)
        at = pl.multiple_of((me ^ (x * sub + s)) * width, LANES)
        out_ref[:, pl.ds(at, width)] = piece[...]


def per_device(tokens, ids, scores, gate_w, up_w, down_w):
    nodes, local, sub = (lax.axis_size(a) for a in ("node", "local", "sub"))
    rows, features = tokens.shape
    local_experts, _, depth = gate_w.shape
    width = down_w.shape[2]
    experts = local_experts * nodes
    n_slices = local * sub
    extra = -(-3 * experts // LANES) * LANES
    count = n_slices * nodes * rows

    packed = call(
        functools.partial(pack_kernel, experts),
        jax.ShapeDtypeStruct((rows, features + extra), bf16),
        [in_hbm(tokens), in_hbm(ids), in_hbm(scores)],
        scratch=[
            pltpu.VMEM(ids.shape, ids.dtype),
            pltpu.VMEM(scores.shape, f32),
            pltpu.SemaphoreType.DMA((3,)),
        ],
        spec=HBM,
    )
    early = [swap(packed, local=x) for x in range(1, local)]
    column = [packed] + [swap(packed, node=z) for z in range(1, nodes)]
    order = [4, 1, 3, 2, 0] if nodes == 4 and local == 2 else None
    own, rest = stack(column, early, (gate_w, up_w), order, ((0, None), (1, None)))
    far = [swap(rest, local=x) for x in range(1, local)]

    blocks = [own] + [stack(pair, (), (gate_w,)) for pair in zip(early, far)]
    for s in range(1, sub):
        blocks += [swap(b, sub=s) for b in blocks[:local]]

    units, crossed = [], []
    for e in range(local_experts):
        h = hidden(blocks, gate_w, up_w, e, features)
        units.append(h)
        crossed.append([swap(h, local=x) for x in range(1, local)])

    add = functools.partial(
        down, weights=down_w, tokens=count, local=local, sub=sub, nodes=nodes
    )
    last = local_experts - 1
    parts = [(units[e], 0, e, 0) for e in range(local_experts)]
    parts += [(c, 0, e, x + 1) for e in range(last) for x, c in enumerate(crossed[e])]
    total = add(parts, last=None, final=False)
    passed = [
        (swap(array, sub=s), 0, e, s * local + x) for s in range(1, sub) for array, _, e, x in parts
    ]
    joined = stack(crossed[last], [total])
    ends = [(joined, (x - 1) * count, last, x) for x in range(1, local)]
    total = add(passed + ends, last=total, final=False)
    ends = [
        (got, at, e, s * local + x)
        for s in range(1, sub)
        for got in [swap(joined, sub=s)]
        for _, at, e, x in ends
    ]
    sent = add(ends, last=total, final=True)

    arrived = [sent[0]] + [swap(sent[z], node=z) for z in range(1, nodes)]
    order = [3, 1, 2, 0] if nodes == 4 else range(nodes)
    pieces = list(add_up([arrived[z] for z in order], rows, n_slices))
    for r in range(1, n_slices):
        s, x = divmod(r, local)
        by = {a: k for a, k in (("local", x), ("sub", s)) if k}
        pieces[r] = swap(pieces[r], **by)
    if width % LANES == 0:
        shape = jax.ShapeDtypeStruct((rows, features), bf16)
        order = [0, 3, 1, 2] if n_slices == 4 else range(n_slices)
        kernel = functools.partial(place_kernel, local, sub, order)
        return call(kernel, shape, [pieces[r] for r in order])
    me = lax.axis_index("local") * sub + lax.axis_index("sub")
    out = jnp.zeros((rows, features), bf16)
    for r, piece in enumerate(pieces):
        s, x = divmod(r, local)
        out = lax.dynamic_update_slice(out, piece, (0, (me ^ (x * sub + s)) * width))
    return out


def solution(mesh):
    everything = P(("groups", "node", "local", "sub"), None)
    weights = P("node", None, ("local", "sub"))
    return jax.shard_map(
        per_device,
        mesh=mesh,
        in_specs=(everything,) * 3 + (weights,) * 3,
        out_specs=everything,
        check_vma=False,
    )
```

```python
import functools

import jax
import jax.numpy as jnp
from jax import lax
from jax.experimental import pallas as pl
from jax.experimental.pallas import tpu as pltpu
from jax.sharding import PartitionSpec as P

route_scale = 2.827
LANES = 128
f32, bf16 = jnp.float32, jnp.bfloat16
VMEM = pl.BlockSpec(memory_space=pltpu.VMEM)
HBM = pl.BlockSpec(memory_space=pltpu.HBM)


def swap(x, **by):
    axes = tuple(by)
    sizes = [lax.axis_size(a) for a in axes]
    pairs = []
    for i in range(functools.reduce(lambda a, b: a * b, sizes)):
        rest, at, to, stride = i, [], 0, 1
        for size, k in zip(sizes[::-1], list(by.values())[::-1]):
            to += ((rest % size) ^ k) * stride
            stride *= size
            rest //= size
        pairs.append((i, to))
    return lax.ppermute(x, axes if len(axes) > 1 else axes[0], pairs)


def in_hbm(x):
    return pltpu.with_memory_space_constraint(x, pltpu.HBM)


def call(kernel, out_shape, args, beside=(), scratch=(), spec=VMEM, flops=0, size=0, vmem=4):
    n = len(args)

    def body(*refs):
        kernel(*refs[:n], *refs[n + len(beside) :])

    return pl.pallas_call(
        body,
        out_shape=out_shape,
        in_specs=[spec] * n + [HBM] * len(beside),
        out_specs=jax.tree.map(lambda _: VMEM, out_shape),
        scratch_shapes=scratch,
        compiler_params=pltpu.CompilerParams(vmem_limit_bytes=vmem << 20),
        cost_estimate=pl.CostEstimate(flops=flops, bytes_accessed=size, transcendentals=0)
        if size
        else None,
    )(*args, *[in_hbm(b) for b in beside])


def pack_kernel(experts, tok_hbm, ids_hbm, scores_hbm, out_ref, ids_ref, scores_ref, sems):
    rows, features = tok_hbm.shape
    extra = out_ref.shape[1] - features
    pairs = ((ids_hbm, ids_ref), (scores_hbm, scores_ref), (tok_hbm, out_ref.at[:, :features]))
    copies = [pltpu.make_async_copy(a, b, sems.at[i]) for i, (a, b) in enumerate(pairs)]
    for copy in copies:
        copy.start()
    copies[0].wait()
    copies[1].wait()
    gate = 1.0 / (1.0 + jnp.exp(-scores_ref[...]))
    share = route_scale * gate / jnp.sum(gate, axis=1, keepdims=True)
    column = lax.broadcasted_iota(jnp.int32, (rows, extra), 1)
    expert, term = column % experts, column // experts
    weight = jnp.zeros((rows, extra), f32)
    for k in range(ids_ref.shape[1]):
        weight += jnp.where(ids_ref[:, k : k + 1] == expert, share[:, k : k + 1], 0.0)
    first = weight.astype(bf16).astype(f32)
    second = (weight - first).astype(bf16).astype(f32)
    third = weight - first - second
    terms = jnp.where(term == 0, first, jnp.where(term == 1, second, jnp.where(term == 2, third, 0.0)))
    out_ref[:, features:] = terms.astype(bf16)
    copies[2].wait()


def stack(parts, after=(), beside=(), order=None, cuts=((0, None),)):
    operands = [*parts, *after]
    order = list(range(len(operands))) if order is None else order
    spans = [parts[first:end] for first, end in cuts]

    def kernel(*refs):
        for (first, _), span, out in zip(cuts, spans, refs[len(operands) :]):
            at = 0
            for i in range(first, first + len(span)):
                ref = refs[order.index(i)]
                rows = ref.shape[0]
                out[at : at + rows, :] = ref[...]
                at += rows

    width, kind = parts[0].shape[1], parts[0].dtype
    shapes = [jax.ShapeDtypeStruct((sum(p.shape[0] for p in span), width), kind) for span in spans]
    out = call(kernel, shapes, [operands[i] for i in order], beside)
    return out if len(cuts) > 1 else out[0]


def hidden(blocks, gate_w, up_w, e, features):
    n = len(blocks)
    local_experts, _, depth = gate_w.shape
    count = sum(b.shape[0] for b in blocks)

    def kernel(*refs):
        *ins, gate_ref, up_ref, out_ref = refs
        experts = local_experts * lax.axis_size("node")
        x = jnp.concatenate([b[:, :features] for b in ins], axis=0)
        tail = jnp.concatenate([b[:, features:] for b in ins], axis=0).astype(f32)
        column = lax.broadcasted_iota(jnp.int32, tail.shape, 1)
        mine = lax.axis_index("node") * local_experts + e
        keep = (column % experts == mine) & (column < 3 * experts)
        weight = jnp.sum(jnp.where(keep, tail, 0.0), axis=1, keepdims=True)
        gate = jnp.dot(x, gate_ref[e], preferred_element_type=f32)
        up = jnp.dot(x, up_ref[e], preferred_element_type=f32)
        out_ref[...] = (gate / (1.0 + jnp.exp(-gate)) * up * weight).astype(bf16)

    return call(
        kernel,
        jax.ShapeDtypeStruct((count, depth), bf16),
        [*blocks, gate_w, up_w],
        flops=4 * count * features * depth,
        size=4 * features * depth,
        vmem=32 if count > 128 else 4,
    )


def down(terms, weights, last, tokens, local, sub, nodes, final):
    n_slices = local * sub
    arrays = []
    for term in terms:
        if not any(term[0] is a for a in arrays):
            arrays.append(term[0])
    index = [next(i for i, a in enumerate(arrays) if a is term[0]) for term in terms]
    depth = weights.shape[1] // n_slices
    width = weights.shape[2]
    block = tokens // n_slices
    rows = block // nodes
    before = [] if last is None else [last]

    def kernel(*refs):
        ins, down_ref = refs[: len(arrays)], refs[len(arrays)]
        outs = refs[len(arrays) + 1 + len(before) :]
        me = lax.axis_index("local") * sub + lax.axis_index("sub")
        total = refs[len(arrays) + 1][...] if before else None
        for i, (_, at, e, r) in zip(index, terms):
            s, x = divmod(r, local)
            here = pl.ds(pl.multiple_of((me ^ (x * sub + s)) * depth, depth), depth)
            h = [ins[i][pl.ds(at + (b ^ r) * block, block), :] for b in range(n_slices)]
            product = jnp.dot(
                jnp.concatenate(h, axis=0), down_ref[e, here, :], preferred_element_type=f32
            )
            total = product if total is None else total + product
        if not final:
            outs[0][...] = total
            return
        for z in range(nodes):
            starts = [b * block + z * rows for b in range(n_slices)]
            outs[z][...] = jnp.concatenate([total[a : a + rows] for a in starts], axis=0).astype(bf16)

    shape = (
        [jax.ShapeDtypeStruct((n_slices * rows, width), bf16)] * nodes
        if final
        else jax.ShapeDtypeStruct((tokens, width), f32)
    )
    return call(
        kernel,
        shape,
        [*arrays, weights, *before],
        flops=2 * len(terms) * tokens * depth * width,
        size=2 * len(terms) * depth * width,
        vmem=32 if tokens > 256 else 4,
    )


def add_up(parts, rows, n_slices):
    def kernel(*refs):
        ins, outs = refs[: len(parts)], refs[len(parts) :]
        total = ins[0][...].astype(f32)
        for ref in ins[1:]:
            total += ref[...].astype(f32)
        for r, out in enumerate(outs):
            out[...] = total[r * rows : (r + 1) * rows].astype(bf16)

    shape = jax.ShapeDtypeStruct((rows, parts[0].shape[1]), bf16)
    return call(kernel, [shape] * n_slices, parts)


def place_kernel(local, sub, order, *refs):
    *pieces, out_ref = refs
    me = lax.axis_index("local") * sub + lax.axis_index("sub")
    width = pieces[0].shape[1]
    for r, piece in zip(order, pieces):
        s, x = divmod(r, local)
        at = pl.multiple_of((me ^ (x * sub + s)) * width, LANES)
        out_ref[:, pl.ds(at, width)] = piece[...]


def per_device(tokens, ids, scores, gate_w, up_w, down_w):
    nodes, local, sub = (lax.axis_size(a) for a in ("node", "local", "sub"))
    rows, features = tokens.shape
    local_experts, _, depth = gate_w.shape
    width = down_w.shape[2]
    experts = local_experts * nodes
    n_slices = local * sub
    extra = -(-3 * experts // LANES) * LANES
    count = n_slices * nodes * rows

    packed = call(
        functools.partial(pack_kernel, experts),
        jax.ShapeDtypeStruct((rows, features + extra), bf16),
        [in_hbm(tokens), in_hbm(ids), in_hbm(scores)],
        scratch=[
            pltpu.VMEM(ids.shape, ids.dtype),
            pltpu.VMEM(scores.shape, f32),
            pltpu.SemaphoreType.DMA((3,)),
        ],
        spec=HBM,
    )
    CROSS = 1 if sub > 1 else 0
    early = [swap(packed, local=x) for x in range(1, local)]
    column = [packed] + [swap(packed, node=z) for z in range(1, nodes)]
    order = [4, 1, 3, 2, 0] if nodes == 4 and local == 2 else None
    own, rest = stack(column, early, (gate_w, up_w), order, ((0, None), (1, None)))
    far = [swap(rest, local=x) for x in range(1, local)]

    blocks = [own] + [stack(pair, (), (gate_w,)) for pair in zip(early, far)]
    for s in range(1, sub):
        blocks += [swap(b, sub=s) for b in blocks[:local]]

    units, crossed = [], []
    for e in range(local_experts):
        h = hidden(blocks, gate_w, up_w, e, features)
        units.append(h)
        crossed.append([swap(h, local=x, sub=CROSS) for x in range(1, local)])

    add = functools.partial(
        down, weights=down_w, tokens=count, local=local, sub=sub, nodes=nodes
    )
    last = local_experts - 1
    def via(x):
        return CROSS * local + x if x else 0

    def term(array, at, e, r):
        return (array, at, e, r)

    parts = [(units[e], 0, e, 0) for e in range(local_experts)]
    parts += [(c, 0, e, via(x + 1)) for e in range(last) for x, c in enumerate(crossed[e])]
    total = add(parts, last=None, final=False)
    passed = [
        (swap(array if r else stack([array], [total]), sub=s), 0, e, r ^ (s * local))
        for s in range(1, sub)
        for array, _, e, r in parts
    ]
    joined = stack(crossed[last], [total])
    ends = [(joined, (x - 1) * count, last, via(x)) for x in range(1, local)]
    total = add(passed + ends, last=total, final=False)
    ends = [
        (got, at, e, r ^ (s * local))
        for s in range(1, sub)
        for got in [swap(joined, sub=s)]
        for _, at, e, r in ends
    ]
    sent = add(ends, last=total, final=True)

    arrived = [sent[0]] + [swap(sent[z], node=z) for z in range(1, nodes)]
    order = [3, 1, 2, 0] if nodes == 4 else range(nodes)
    pieces = list(add_up([arrived[z] for z in order], rows, n_slices))
    for r in range(1, n_slices):
        s, x = divmod(r, local)
        by = {a: k for a, k in (("local", x), ("sub", s)) if k}
        pieces[r] = swap(pieces[r], **by)
    if width % LANES == 0:
        shape = jax.ShapeDtypeStruct((rows, features), bf16)
        order = [0, 3, 1, 2] if n_slices == 4 else range(n_slices)
        kernel = functools.partial(place_kernel, local, sub, order)
        return call(kernel, shape, [pieces[r] for r in order])
    me = lax.axis_index("local") * sub + lax.axis_index("sub")
    out = jnp.zeros((rows, features), bf16)
    for r, piece in enumerate(pieces):
        s, x = divmod(r, local)
        out = lax.dynamic_update_slice(out, piece, (0, (me ^ (x * sub + s)) * width))
    return out


def solution(mesh):
    everything = P(("groups", "node", "local", "sub"), None)
    weights = P("node", None, ("local", "sub"))
    return jax.shard_map(
        per_device,
        mesh=mesh,
        in_specs=(everything,) * 3 + (weights,) * 3,
        out_specs=everything,
        check_vma=False,
    )
```
